1024 devices in a mesh: ep: 16 (over z, core), rep: 8 (over y), opt: 8 (over x).
Axes of the slice: x: 8, y: 8, z: 8, core: 2. Of those that a mesh axis runs over, the one named last changes fastest.
Arguments:
- incoming_tokens: bfloat16 [16, 8, 8, 128, 2048], P('ep', 'rep', None, None, 'opt'), may hold values from -6 to 6
- cotangent: bfloat16 [16, 8, 8, 128, 2048], P('ep', 'rep', None, None, 'opt'), may hold values from -6 to 6
- block_dest: int32 [16, 8, 8], replicated, may hold values from 0 to 15, as said below
- gate_weight: bfloat16 [16, 2048, 768], P('ep'), may hold values from -0.125 to 0.125
- up_weight: bfloat16 [16, 2048, 768], P('ep'), may hold values from -0.125 to 0.125
- basis: bfloat16 [16, 768, 512], P('ep'), may hold values from -0.21875 to 0.21875
- moment_first: float32 [16, 512, 2048], P('ep', 'rep', 'opt'), may hold values from -6 to 6
- moment_second: float32 [16, 512, 2048], P('ep', 'rep', 'opt'), may hold values from 0.05 to 1
Outputs:
- first_moment: float32 [16, 512, 2048], P('ep', 'rep', 'opt')
- second_moment: float32 [16, 512, 2048], P('ep', 'rep', 'opt')
- weight_delta: bfloat16 [16, 768, 2048], P('ep', None, 'opt')
The draws below stay inside these ranges and needn't reach their ends.
Inputs may be any that keep to these rules, and one draw needn't show every extreme that they name: `block_dest`: the 8 blocks of one pair of indices (s, r) go to 8 different instances.
All inputs are finite; a program needn't handle non-finite values.
Results may differ from the reference program's by a relative error of at most 0.0085.
Values may be sent and summed in bfloat16 or wider, within the bound.
A program may use at most 32 MiB of HBM per device.

```python
import math
import jax
import jax.numpy as jnp
from jax import lax

D = 2048
FF = 768
RANK = 512
BLOCK_ROWS = 128
INSTANCES = 16
REPLICAS = 8
BLOCKS = 8
N_EP = 16
N_REP = 8


def draw_block_dest(key, part):
    heat_key, score_key = jax.random.split(jax.random.fold_in(key, 17))
    instance_heat = jax.random.randint(heat_key, (N_EP,), 0, 4) * 512
    scores = jax.random.randint(score_key, (N_EP, N_REP, N_EP), 0, 1024) + instance_heat[None, None, :]
    distinct = scores * N_EP + jnp.arange(N_EP, dtype=jnp.int32)[None, None, :]
    return lax.top_k(distinct, BLOCKS)[1].astype(jnp.int32)


def block_scale(stream_key, extent, pieces, least, high):
    loudness = 1.0
    for axis_at, shards_of in pieces:
        draws = jax.random.uniform(jax.random.fold_in(jax.random.fold_in(stream_key, 6), axis_at), (shards_of,), jnp.float32, least / len(pieces), high / len(pieces))
        loudness = loudness * jnp.repeat(jnp.exp(draws), extent[axis_at] // shards_of).reshape((-1,) + (1,) * (len(extent) - 1 - axis_at))
    return loudness


def normal_values(own_key, extent, width, reach, shards=(), held_as=jnp.bfloat16):
    result = width * jax.random.normal(own_key, extent, jnp.float32)
    if shards:
        result = result * block_scale(own_key, extent, shards, -0.22, 0.18)
    return jnp.clip(result, -reach, reach).astype(held_as)


def setup_inputs(seed: int = 0) -> dict:
    seeds = jax.random.split(jax.random.key(seed), 9)
    incoming_tokens = normal_values(seeds[0], (INSTANCES, REPLICAS, BLOCKS, BLOCK_ROWS, D), 1.0, 6.0, ((0, 16), (1, 8), (4, 8)))
    cotangent = normal_values(seeds[1], (INSTANCES, REPLICAS, BLOCKS, BLOCK_ROWS, D), 1.0, 6.0, ((0, 16), (1, 8), (4, 8)))
    block_dest = draw_block_dest(jax.random.fold_in(seeds[8], 71), 0)
    gate_weight = normal_values(seeds[3], (INSTANCES, D, FF), D ** -0.5, 0.125, ((0, 16),))
    up_weight = normal_values(seeds[4], (INSTANCES, D, FF), D ** -0.5, 0.125, ((0, 16),))
    basis = normal_values(seeds[5], (INSTANCES, FF, RANK), FF ** -0.5, 0.21875, ((0, 16),))
    moment_first = normal_values(seeds[6], (INSTANCES, RANK, D), 1.0, 6.0, ((0, 16), (1, 8), (2, 8)), jnp.float32)
    moment_second = jnp.clip(jnp.exp(math.log(1.0) - 2.9957323 * jax.random.uniform(seeds[7], (INSTANCES, RANK, D), jnp.float32) ** block_scale(seeds[7], (INSTANCES, RANK, D), ((0, 16), (1, 8), (2, 8)), -0.2, 0.2)), 0.05, 1.0)
    return dict(incoming_tokens=incoming_tokens, cotangent=cotangent, block_dest=block_dest, gate_weight=gate_weight, up_weight=up_weight, basis=basis, moment_first=moment_first, moment_second=moment_second)


beta_one = 0.9
beta_two = 0.999
adam_step = 1000.0
adam_eps = 1e-08

def reference(incoming_tokens, cotangent, block_dest, gate_weight, up_weight, basis, moment_first, moment_second):
    flat_tokens = incoming_tokens.reshape(-1, BLOCK_ROWS, D)
    flat_cotangent = cotangent.reshape(-1, BLOCK_ROWS, D)
    flat_dest = block_dest.reshape(-1).astype(jnp.int32)

    def accumulate(running_total, item):
        block_tokens, block_cotangent, target_value = item
        gate_values = jnp.dot(block_tokens, gate_weight[target_value], preferred_element_type=jnp.float32)
        up_values = jnp.dot(block_tokens, up_weight[target_value], preferred_element_type=jnp.float32)
        hidden = (jax.nn.silu(gate_values) * up_values).astype(jnp.bfloat16)
        projected = jnp.dot(hidden, basis[target_value], preferred_element_type=jnp.float32).astype(jnp.bfloat16)
        contribution = jnp.dot(projected.T, block_cotangent, preferred_element_type=jnp.float32)
        current = lax.dynamic_index_in_dim(running_total, target_value, 0, keepdims=False)
        running_total = lax.dynamic_update_index_in_dim(running_total, current + contribution, target_value, 0)
        return (running_total, None)
    gradients, _ = lax.scan(accumulate, jnp.zeros((N_EP, RANK, D), jnp.float32), (flat_tokens, flat_cotangent, flat_dest))
    first_moment = beta_one * moment_first + (1.0 - beta_one) * gradients
    second_moment = beta_two * moment_second + (1.0 - beta_two) * gradients * gradients
    scaled_first = first_moment / (1.0 - beta_one ** adam_step)
    scaled_second = second_moment / (1.0 - beta_two ** adam_step)
    update = (-scaled_first / (jnp.sqrt(scaled_second) + adam_eps)).astype(jnp.bfloat16)
    weight_change = jnp.einsum('efr,erd->efd', basis.astype(jnp.float32), update.astype(jnp.float32), precision=lax.Precision.HIGHEST)
    return (first_moment, second_moment, weight_change.astype(jnp.bfloat16))
```

```python
import functools

import jax
import jax.numpy as jnp
from jax import lax
from jax.experimental import pallas as pl
from jax.experimental.pallas import tpu as pltpu
from jax.sharding import PartitionSpec as P

beta_one = 0.9
beta_two = 0.999
adam_step = 1000.0
adam_eps = 1e-08

MESH = pl.DeviceIdType.MESH
BF16 = jnp.bfloat16
F32 = jnp.float32

BLOCKS = 8
SUB = 16
CHUNK = 8
RANK = 512
FEAT = 256
MODEL = 2048
FF = 768
OWN = 64

SLOTS = (
    (0, 0), (0, 1), (1, 0), (1, 1), (-1, 0), (-1, 1), (2, 0), (2, 1),
    (-2, 0), (-2, 1), (3, 0), (3, 1), (-3, 0), (-3, 1), (4, 0), (4, 1),
)
TOKEN_ORDER = (2, 4, 3, 5, 6, 7, 1, 14, 15, 10, 12, 11, 13, 8, 9)
COT_FIRST = (10, 12, 11, 13, 2, 4, 3, 5, 1)
COT_LATER = (6, 7, 14, 15, 8, 9)


def kernel(
    dest_ref, tok_hbm, cot_hbm, gate_hbm, up_hbm, basis_hbm, m1_hbm, m2_hbm,
    m1_out, m2_out, delta_out,
    gate_v, up_v, basis_v, basis_t, cot_v, m1_v, m2_v, xtok,
    csend, crecv, tsend, trecv, hidden, pt, grad, gsend, grecv, upd,
    local_sem, xs, xr, cs, cr, ts, tr, ps, pr, gs, gr, us, ur,
):
    e = lax.axis_index("ep")
    r = lax.axis_index("rep")
    o = lax.axis_index("opt")
    z, c = lax.div(e, 2), lax.rem(e, 2)

    def ep_of(q):
        dz, dc = SLOTS[q]
        core = 1 - c if dc else c
        return lax.rem(z + (dz + 8), 8) * 2 + core

    def turn(axis_index, k):
        return lax.rem(axis_index + k, 8)

    own_features = pl.ds(pl.multiple_of(o * FEAT, FEAT), FEAT)
    loads = [
        pltpu.make_async_copy(cot_hbm, cot_v, local_sem.at[0]),
        pltpu.make_async_copy(tok_hbm.at[:, o], xtok.at[:, :, own_features], local_sem.at[1]),
        pltpu.make_async_copy(basis_hbm.at[0], basis_v, local_sem.at[2]),
        pltpu.make_async_copy(gate_hbm.at[0], gate_v, local_sem.at[3]),
        pltpu.make_async_copy(up_hbm.at[0], up_v, local_sem.at[4]),
        pltpu.make_async_copy(m1_hbm.at[0], m1_v, local_sem.at[5]),
        pltpu.make_async_copy(m2_hbm.at[0], m2_v, local_sem.at[6]),
    ]
    for load in loads:
        load.start()

    barrier = pltpu.get_barrier_semaphore()
    for k in range(1, 8):
        pl.semaphore_signal(barrier, inc=1, device_id={"opt": turn(o, k)}, device_id_type=MESH)
        pl.semaphore_signal(barrier, inc=1, device_id={"rep": turn(r, k)}, device_id_type=MESH)
    for q in range(1, 16):
        pl.semaphore_signal(barrier, inc=1, device_id={"ep": ep_of(q)}, device_id_type=MESH)
    pl.semaphore_wait(barrier, 29)

    def x_copy(k):
        return pltpu.make_async_remote_copy(
            src_ref=tok_hbm.at[:, turn(o, k)],
            dst_ref=xtok.at[:, :, own_features],
            send_sem=xs.at[k],
            recv_sem=xr.at[k],
            device_id={"opt": turn(o, k)},
            device_id_type=MESH,
        )

    x_copies = [x_copy(k) for k in range(1, 8)]
    for copy in x_copies:
        copy.start()

    dest = [dest_ref[r, b, e] for b in range(BLOCKS)]

    def block_for(q):
        target = ep_of(q)
        index, found = jnp.int32(0), jnp.int32(0)
        for b in range(BLOCKS):
            hit = dest[b] == target
            index = jnp.where(hit, b, index)
            found = jnp.where(hit, 1, found)
        return index, found

    def cot_copy(q):
        return pltpu.make_async_remote_copy(
            src_ref=csend.at[q],
            dst_ref=crecv.at[q // CHUNK, :, q % CHUNK],
            send_sem=cs.at[q],
            recv_sem=cr.at[q],
            device_id={"ep": ep_of(q)},
            device_id_type=MESH,
        )

    def token_copy(q):
        return pltpu.make_async_remote_copy(
            src_ref=tsend.at[q],
            dst_ref=trecv.at[q // CHUNK, q % CHUNK],
            send_sem=ts.at[q],
            recv_sem=tr.at[q],
            device_id={"ep": ep_of(q)},
            device_id_type=MESH,
        )

    def send_cot(q):
        index, _ = block_for(q)
        csend[q] = cot_v[index]
        cot_copy(q).start()

    def token_slot(q):
        index, found = block_for(q)
        rows = xtok[index]
        return jnp.where(found > 0, rows, jnp.zeros_like(rows))

    loads[0].wait()
    for q in COT_FIRST:
        send_cot(q)
    crecv[0, :, 0] = cot_v[block_for(0)[0]]

    loads[2].wait()
    for part in range(3):
        rows = pl.ds(part * 256, 256)
        basis_t[:, rows] = basis_v[rows, :].T

    loads[1].wait()
    for copy in x_copies:
        copy.wait_recv()
    for q in TOKEN_ORDER:
        tsend[q] = token_slot(q)
        token_copy(q).start()
    trecv[0, 0] = token_slot(0)

    loads[3].wait()
    loads[4].wait()

    own_columns = pl.ds(pl.multiple_of(o * 128, 128), 128)

    def pt_copy(chunk, k):
        return pltpu.make_async_remote_copy(
            src_ref=pt.at[chunk, :, own_columns],
            dst_ref=pt.at[chunk, :, own_columns],
            send_sem=ps.at[chunk, k],
            recv_sem=pr.at[chunk, k],
            device_id={"opt": turn(o, k)},
            device_id_type=MESH,
        )

    def project(chunk):
        rows = trecv[chunk].reshape(CHUNK * SUB, MODEL)
        for part in range(3):
            columns = pl.ds(part * 256, 256)
            gate = jnp.dot(rows, gate_v[:, columns], preferred_element_type=F32)
            up = jnp.dot(rows, up_v[:, columns], preferred_element_type=F32)
            hidden[:, columns] = (gate / (1.0 + jnp.exp(-gate)) * up).astype(BF16)
        projected = lax.dot_general(
            basis_t[...], hidden[...], (((1,), (1,)), ((), ())), preferred_element_type=F32
        )
        pt[chunk, :, own_columns] = projected.astype(BF16)
        for k in range(1, 8):
            pt_copy(chunk, k).start()

    for q in range(1, CHUNK):
        token_copy(q).wait_recv()
    project(0)
    for q in COT_LATER:
        send_cot(q)
    for q in range(CHUNK, 2 * CHUNK):
        token_copy(q).wait_recv()
    project(1)

    def contract(chunk):
        return jnp.dot(
            pt[chunk],
            crecv[chunk].reshape(8 * CHUNK * SUB, FEAT),
            preferred_element_type=F32,
        )

    for q in range(1, CHUNK):
        cot_copy(q).wait_recv()
    for k in range(1, 8):
        pt_copy(0, k).wait_recv()
    grad[...] = contract(0)
    for q in range(CHUNK, 2 * CHUNK):
        cot_copy(q).wait_recv()
    for k in range(1, 8):
        pt_copy(1, k).wait_recv()
    grad[...] += contract(1)
    gsend[...] = grad[...].astype(BF16)

    def grad_copy(k):
        rows = pl.ds(pl.multiple_of(turn(r, k) * OWN, OWN), OWN)
        return pltpu.make_async_remote_copy(
            src_ref=gsend.at[rows],
            dst_ref=grecv.at[k],
            send_sem=gs.at[k],
            recv_sem=gr.at[k],
            device_id={"rep": turn(r, k)},
            device_id_type=MESH,
        )

    for k in (4, 3, 5, 2, 6, 1, 7):
        grad_copy(k).start()
    own_rows = pl.ds(pl.multiple_of(r * OWN, OWN), OWN)
    gradient = grad[own_rows, :]
    loads[5].wait()
    loads[6].wait()
    for k in range(1, 8):
        grad_copy(k).wait_recv()
    for k in range(1, 8):
        gradient += grecv[k].astype(F32)

    first_moment = beta_one * m1_v[...] + (1.0 - beta_one) * gradient
    second_moment = beta_two * m2_v[...] + (1.0 - beta_two) * gradient * gradient
    m1_out[0] = first_moment
    m2_out[0] = second_moment
    scaled_first = first_moment / (1.0 - beta_one**adam_step)
    scaled_second = second_moment / (1.0 - beta_two**adam_step)
    upd[own_rows, :] = (-scaled_first / (jnp.sqrt(scaled_second) + adam_eps)).astype(BF16)

    def update_copy(k):
        return pltpu.make_async_remote_copy(
            src_ref=upd.at[own_rows],
            dst_ref=upd.at[own_rows],
            send_sem=us.at[k],
            recv_sem=ur.at[k],
            device_id={"rep": turn(r, k)},
            device_id_type=MESH,
        )

    for k in (4, 3, 5, 2, 6, 1, 7):
        update_copy(k).start()
    for copy in x_copies:
        copy.wait_send()
    for q in range(1, 16):
        cot_copy(q).wait_send()
        token_copy(q).wait_send()
    for k in range(1, 8):
        pt_copy(0, k).wait_send()
        pt_copy(1, k).wait_send()
        grad_copy(k).wait_send()
    for k in range(1, 8):
        update_copy(k).wait_recv()
    delta_out[0] = jnp.dot(basis_v[...], upd[...], preferred_element_type=F32).astype(BF16)
    for k in range(1, 8):
        update_copy(k).wait_send()


def shards(
    incoming_tokens,
    cotangent,
    block_dest,
    gate_weight,
    up_weight,
    basis,
    moment_first,
    moment_second,
):
    tokens = incoming_tokens.reshape(BLOCKS, 8, SUB, FEAT)
    cot = cotangent.reshape(BLOCKS, 8, SUB, FEAT)
    hbm = pl.BlockSpec(memory_space=pl.ANY)
    vmem = pl.BlockSpec(memory_space=pltpu.VMEM)
    dma = pltpu.SemaphoreType.DMA
    return pl.pallas_call(
        kernel,
        out_shape=(
            jax.ShapeDtypeStruct((1, OWN, FEAT), F32),
            jax.ShapeDtypeStruct((1, OWN, FEAT), F32),
            jax.ShapeDtypeStruct((1, FF, FEAT), BF16),
        ),
        in_specs=[pl.BlockSpec(memory_space=pltpu.SMEM)] + [hbm] * 7,
        out_specs=(vmem, vmem, vmem),
        scratch_shapes=[
            pltpu.VMEM((MODEL, FF), BF16),
            pltpu.VMEM((MODEL, FF), BF16),
            pltpu.VMEM((FF, RANK), BF16),
            pltpu.VMEM((RANK, FF), BF16),
            pltpu.VMEM((BLOCKS, 8, SUB, FEAT), BF16),
            pltpu.VMEM((OWN, FEAT), F32),
            pltpu.VMEM((OWN, FEAT), F32),
            pltpu.VMEM((BLOCKS, SUB, MODEL), BF16),
            pltpu.VMEM((16, 8, SUB, FEAT), BF16),
            pltpu.VMEM((2, 8, CHUNK, SUB, FEAT), BF16),
            pltpu.VMEM((16, SUB, MODEL), BF16),
            pltpu.VMEM((2, CHUNK, SUB, MODEL), BF16),
            pltpu.VMEM((CHUNK * SUB, FF), BF16),
            pltpu.VMEM((2, RANK, 8 * CHUNK * SUB), BF16),
            pltpu.VMEM((RANK, FEAT), F32),
            pltpu.VMEM((RANK, FEAT), BF16),
            pltpu.VMEM((8, OWN, FEAT), BF16),
            pltpu.VMEM((RANK, FEAT), BF16),
            dma((7,)),
            dma((8,)), dma((8,)),
            dma((16,)), dma((16,)),
            dma((16,)), dma((16,)),
            dma((2, 8)), dma((2, 8)),
            dma((8,)), dma((8,)),
            dma((8,)), dma((8,)),
        ],
        compiler_params=pltpu.CompilerParams(
            collective_id=0, has_side_effects=True, vmem_limit_bytes=63 * 1024 * 1024
        ),
    )(jnp.transpose(block_dest, (1, 2, 0)), tokens, cot, gate_weight, up_weight, basis, moment_first, moment_second)


def solution(mesh):
    in_specs = (
        P("ep", "rep", None, None, "opt"),
        P("ep", "rep", None, None, "opt"),
        P(),
        P("ep", None, None),
        P("ep", None, None),
        P("ep", None, None),
        P("ep", "rep", "opt"),
        P("ep", "rep", "opt"),
    )
    out_specs = (P("ep", "rep", "opt"), P("ep", "rep", "opt"), P("ep", None, "opt"))
    return jax.shard_map(shards, mesh=mesh, in_specs=in_specs, out_specs=out_specs, check_vma=False)
```

```python
import functools

import jax
import jax.numpy as jnp
from jax import lax
from jax.experimental import pallas as pl
from jax.experimental.pallas import tpu as pltpu
from jax.sharding import PartitionSpec as P

beta_one = 0.9
beta_two = 0.999
adam_step = 1000.0
adam_eps = 1e-08

MESH = pl.DeviceIdType.MESH
BF16 = jnp.bfloat16
F32 = jnp.float32

BLOCKS = 8
SUB = 16
RANK = 512
FEAT = 256
MODEL = 2048
FF = 768
OWN = 64

SLOTS = (
    (0, 0), (0, 1), (1, 0), (1, 1), (-1, 0), (-1, 1),
    (2, 0), (2, 1), (-2, 0), (-2, 1),
    (3, 0), (3, 1), (-3, 0), (-3, 1),
    (4, 0), (4, 1),
)
CHUNKS = ((0, 6), (6, 10), (10, 14), (14, 16))
LAST = len(CHUNKS) - 1
PLACE = {q: (n, q - low) for n, (low, high) in enumerate(CHUNKS) for q in range(low, high)}
TOKEN_ORDER = (2, 4, 3, 5, 1, 6, 8, 7, 9, 10, 12, 11, 13, 14, 15)
COT_FIRST = (10, 12, 11, 13, 2, 4, 3, 5, 1)
COT_LATER = (6, 8, 7, 9, 14, 15)
DIRECT = (1, 7, 2, 6)
DIRECT_ALL = (4, 3, 5, 2, 6, 1, 7)


def adam(moment_first, moment_second, gradient):
    first_moment = beta_one * moment_first + (1.0 - beta_one) * gradient
    second_moment = beta_two * moment_second + (1.0 - beta_two) * gradient * gradient
    scaled_first = first_moment / (1.0 - beta_one**adam_step)
    scaled_second = second_moment / (1.0 - beta_two**adam_step)
    update = (-scaled_first / (jnp.sqrt(scaled_second) + adam_eps)).astype(BF16)
    return first_moment, second_moment, update


def rows_of(chunk):
    low, high = CHUNKS[chunk]
    return (high - low) * SUB


def kernel(
    dest_ref, tok_hbm, cot_hbm, gate_hbm, up_hbm, basis_hbm, m1_hbm, m2_hbm,
    gradient_out, update_out,
    gate_v, up_v, basis_v, cot_v, m1_v, m2_v, xtok, csend, tsend, hidden, grad, gsend, grecv, upd,
    crecv, trecv, proj,
    local_sem, xs, xr, cs, cr, ts, tr, ps, pr, gs, gr, us, ur,
):
    e = lax.axis_index("ep")
    r = lax.axis_index("rep")
    o = lax.axis_index("opt")
    z, c = lax.div(e, 2), lax.rem(e, 2)

    def ep_of(q):
        dz, dc = SLOTS[q]
        core = 1 - c if dc else c
        return lax.rem(z + (dz + 8), 8) * 2 + core

    def turn(axis_index, k):
        return lax.rem(axis_index + k, 8)

    own_features = pl.ds(pl.multiple_of(o * FEAT, FEAT), FEAT)
    loads = [
        pltpu.make_async_copy(cot_hbm, cot_v, local_sem.at[0]),
        pltpu.make_async_copy(tok_hbm.at[:, o], xtok.at[:, :, own_features], local_sem.at[1]),
        pltpu.make_async_copy(basis_hbm.at[0], basis_v, local_sem.at[2]),
        pltpu.make_async_copy(gate_hbm.at[0], gate_v, local_sem.at[3]),
        pltpu.make_async_copy(up_hbm.at[0], up_v, local_sem.at[4]),
        pltpu.make_async_copy(m1_hbm.at[0], m1_v, local_sem.at[5]),
        pltpu.make_async_copy(m2_hbm.at[0], m2_v, local_sem.at[6]),
    ]
    for load in loads:
        load.start()

    barrier = pltpu.get_barrier_semaphore()
    for k in range(1, 8):
        pl.semaphore_signal(barrier, inc=1, device_id={"opt": turn(o, k)}, device_id_type=MESH)
        pl.semaphore_signal(barrier, inc=1, device_id={"rep": turn(r, k)}, device_id_type=MESH)
    for q in range(1, 16):
        pl.semaphore_signal(barrier, inc=1, device_id={"ep": ep_of(q)}, device_id_type=MESH)
    pl.semaphore_wait(barrier, 29)

    def x_copy(k):
        return pltpu.make_async_remote_copy(
            src_ref=tok_hbm.at[:, turn(o, k)],
            dst_ref=xtok.at[:, :, own_features],
            send_sem=xs.at[k],
            recv_sem=xr.at[k],
            device_id={"opt": turn(o, k)},
            device_id_type=MESH,
        )

    x_copies = [x_copy(k) for k in range(1, 8)]
    for copy in x_copies:
        copy.start()

    dest = [dest_ref[r, b, e] for b in range(BLOCKS)]

    def block_for(q):
        target = ep_of(q)
        index, found = jnp.int32(0), jnp.int32(0)
        for b in range(BLOCKS):
            hit = dest[b] == target
            index = jnp.where(hit, b, index)
            found = jnp.where(hit, 1, found)
        return index, found

    def cot_copy(q):
        return pltpu.make_async_remote_copy(
            src_ref=csend.at[q],
            dst_ref=crecv[PLACE[q][0]].at[:, PLACE[q][1]],
            send_sem=cs.at[q],
            recv_sem=cr.at[q],
            device_id={"ep": ep_of(q)},
            device_id_type=MESH,
        )

    def token_copy(q):
        return pltpu.make_async_remote_copy(
            src_ref=tsend.at[q],
            dst_ref=trecv[PLACE[q][0]].at[PLACE[q][1]],
            send_sem=ts.at[q],
            recv_sem=tr.at[q],
            device_id={"ep": ep_of(q)},
            device_id_type=MESH,
        )

    def send_cot(q):
        index, _ = block_for(q)
        csend[q] = cot_v[index]
        cot_copy(q).start()

    def token_slot(q):
        index, found = block_for(q)
        rows = xtok[index]
        return jnp.where(found > 0, rows, jnp.zeros_like(rows))

    loads[0].wait()
    for q in COT_FIRST:
        send_cot(q)
    crecv[0][:, 0] = cot_v[block_for(0)[0]]

    loads[1].wait()
    for copy in x_copies:
        copy.wait_recv()
    for q in TOKEN_ORDER:
        tsend[q] = token_slot(q)
        token_copy(q).start()
    trecv[0][0] = token_slot(0)

    loads[3].wait()
    loads[4].wait()

    loads[2].wait()

    def direct(chunk, k):
        return pltpu.make_async_remote_copy(
            src_ref=proj[chunk].at[o],
            dst_ref=proj[chunk].at[o],
            send_sem=ps.at[chunk, k],
            recv_sem=pr.at[chunk, k],
            device_id={"opt": turn(o, k)},
            device_id_type=MESH,
        )

    def forwards(chunk):
        half = rows_of(chunk) // 2
        moves = (
            (turn(o, 6), 0, 2 * half, 1, 3),
            (turn(o, 2), 0, 2 * half, 7, 5),
            (turn(o, 6), 0, half, 2, 4),
            (turn(o, 2), half, half, 6, 0),
        )
        return [
            pltpu.make_async_remote_copy(
                src_ref=proj[chunk].at[source, pl.ds(low, size)],
                dst_ref=proj[chunk].at[source, pl.ds(low, size)],
                send_sem=ps.at[chunk, sem],
                recv_sem=pr.at[chunk, sem],
                device_id={"opt": turn(o, k)},
                device_id_type=MESH,
            )
            for source, low, size, k, sem in moves
        ]

    def project(chunk):
        for q in range(*CHUNKS[chunk]):
            if q:
                token_copy(q).wait_recv()
        rows = trecv[chunk][...].reshape(rows_of(chunk), MODEL)
        local = pl.ds(0, rows_of(chunk))
        for part in range(3):
            columns = pl.ds(part * 256, 256)
            gate = jnp.dot(rows, gate_v[:, columns], preferred_element_type=F32)
            up = jnp.dot(rows, up_v[:, columns], preferred_element_type=F32)
            hidden[local, columns] = (gate / (1.0 + jnp.exp(-gate)) * up).astype(BF16)
        projected = jnp.dot(hidden[local, :], basis_v[...], preferred_element_type=F32)
        proj[chunk][o] = projected.astype(BF16)

    def send_direct(chunk):
        for k in DIRECT_ALL if chunk == LAST else DIRECT:
            direct(chunk, k).start()

    def pass_on(chunk):
        direct(chunk, 2).wait_recv()
        direct(chunk, 6).wait_recv()
        for copy in forwards(chunk):
            copy.start()

    def contract(chunk):
        for q in range(*CHUNKS[chunk]):
            if q:
                cot_copy(q).wait_recv()
        if chunk == LAST:
            for k in DIRECT_ALL:
                direct(chunk, k).wait_recv()
        else:
            direct(chunk, 1).wait_recv()
            direct(chunk, 7).wait_recv()
            for copy in forwards(chunk):
                copy.wait_recv()
        return lax.dot_general(
            proj[chunk][...].reshape(8 * rows_of(chunk), RANK),
            crecv[chunk][...].reshape(8 * rows_of(chunk), FEAT),
            (((0,), (0,)), ((), ())),
            preferred_element_type=F32,
        )

    project(0)
    send_direct(0)
    project(1)
    pass_on(0)
    send_direct(1)
    for q in COT_LATER:
        send_cot(q)
    project(2)
    pass_on(1)
    send_direct(2)
    project(3)
    send_direct(3)
    pass_on(2)
    grad[...] = contract(0)
    grad[...] += contract(1)
    grad[...] += contract(2)
    grad[...] += contract(3)
    gsend[...] = grad[...].astype(BF16)

    def grad_copy(k):
        rows = pl.ds(pl.multiple_of(turn(r, k) * OWN, OWN), OWN)
        return pltpu.make_async_remote_copy(
            src_ref=gsend.at[rows],
            dst_ref=grecv.at[k],
            send_sem=gs.at[k],
            recv_sem=gr.at[k],
            device_id={"rep": turn(r, k)},
            device_id_type=MESH,
        )

    for k in (4, 3, 5, 2, 6, 1, 7):
        grad_copy(k).start()
    own_rows = pl.ds(pl.multiple_of(r * OWN, OWN), OWN)
    gradient = grad[own_rows, :]
    loads[5].wait()
    loads[6].wait()
    for k in range(1, 8):
        grad_copy(k).wait_recv()
    for k in range(1, 8):
        gradient += grecv[k].astype(F32)

    gradient_out[...] = gradient
    upd[own_rows, :] = adam(m1_v[...], m2_v[...], gradient)[2]

    def update_copy(k):
        return pltpu.make_async_remote_copy(
            src_ref=upd.at[own_rows],
            dst_ref=upd.at[own_rows],
            send_sem=us.at[k],
            recv_sem=ur.at[k],
            device_id={"rep": turn(r, k)},
            device_id_type=MESH,
        )

    for k in (4, 3, 5, 2, 6, 1, 7):
        update_copy(k).start()
    for copy in x_copies:
        copy.wait_send()
    for q in range(1, 16):
        cot_copy(q).wait_send()
        token_copy(q).wait_send()
    for chunk in range(LAST):
        for k in DIRECT:
            direct(chunk, k).wait_send()
        for copy in forwards(chunk):
            copy.wait_send()
    for k in range(1, 8):
        direct(LAST, k).wait_send()
        grad_copy(k).wait_send()
    for k in range(1, 8):
        update_copy(k).wait_recv()
    update_out[...] = upd[...]
    for k in range(1, 8):
        update_copy(k).wait_send()


def finish(gradient_ref, update_ref, basis_ref, m1_ref, m2_ref, m1_out, m2_out, delta_out):
    first_moment, second_moment, _ = adam(m1_ref[0], m2_ref[0], gradient_ref[...])
    m1_out[0] = first_moment
    m2_out[0] = second_moment
    delta_out[0] = jnp.dot(basis_ref[0], update_ref[...], preferred_element_type=F32).astype(BF16)


def shards(
    incoming_tokens,
    cotangent,
    block_dest,
    gate_weight,
    up_weight,
    basis,
    moment_first,
    moment_second,
):
    tokens = incoming_tokens.reshape(BLOCKS, 8, SUB, FEAT)
    cot = cotangent.reshape(BLOCKS, 8, SUB, FEAT)
    hbm = pl.BlockSpec(memory_space=pl.ANY)
    vmem = pl.BlockSpec(memory_space=pltpu.VMEM)
    dma = pltpu.SemaphoreType.DMA
    gradient, update = pl.pallas_call(
        kernel,
        out_shape=(
            jax.ShapeDtypeStruct((OWN, FEAT), F32),
            jax.ShapeDtypeStruct((RANK, FEAT), BF16),
        ),
        in_specs=[pl.BlockSpec(memory_space=pltpu.SMEM)] + [hbm] * 7,
        out_specs=(vmem, vmem),
        scratch_shapes=[
            pltpu.VMEM((MODEL, FF), BF16),
            pltpu.VMEM((MODEL, FF), BF16),
            pltpu.VMEM((FF, RANK), BF16),
            pltpu.VMEM((BLOCKS, 8, SUB, FEAT), BF16),
            pltpu.VMEM((OWN, FEAT), F32),
            pltpu.VMEM((OWN, FEAT), F32),
            pltpu.VMEM((BLOCKS, SUB, MODEL), BF16),
            pltpu.VMEM((16, 8, SUB, FEAT), BF16),
            pltpu.VMEM((16, SUB, MODEL), BF16),
            pltpu.VMEM((rows_of(0), FF), BF16),
            pltpu.VMEM((RANK, FEAT), F32),
            pltpu.VMEM((RANK, FEAT), BF16),
            pltpu.VMEM((8, OWN, FEAT), BF16),
            pltpu.VMEM((RANK, FEAT), BF16),
            [pltpu.VMEM((8, high - low, SUB, FEAT), BF16) for low, high in CHUNKS],
            [pltpu.VMEM((high - low, SUB, MODEL), BF16) for low, high in CHUNKS],
            [pltpu.VMEM((8, (high - low) * SUB, RANK), BF16) for low, high in CHUNKS],
            dma((7,)),
            dma((8,)), dma((8,)),
            dma((16,)), dma((16,)),
            dma((16,)), dma((16,)),
            dma((len(CHUNKS), 8)), dma((len(CHUNKS), 8)),
            dma((8,)), dma((8,)),
            dma((8,)), dma((8,)),
        ],
        compiler_params=pltpu.CompilerParams(
            collective_id=0, has_side_effects=True, vmem_limit_bytes=63 * 1024 * 1024
        ),
    )(
        jnp.transpose(block_dest, (1, 2, 0)),
        tokens,
        cot,
        gate_weight,
        up_weight,
        basis,
        moment_first,
        moment_second,
    )
    return pl.pallas_call(
        finish,
        out_shape=(
            jax.ShapeDtypeStruct((1, OWN, FEAT), F32),
            jax.ShapeDtypeStruct((1, OWN, FEAT), F32),
            jax.ShapeDtypeStruct((1, FF, FEAT), BF16),
        ),
        in_specs=[vmem] * 5,
        out_specs=(vmem, vmem, vmem),
        cost_estimate=pl.CostEstimate(flops=2 * FF * RANK * FEAT, bytes_accessed=2**21, transcendentals=0),
    )(gradient, update, basis, moment_first, moment_second)


def solution(mesh):
    in_specs = (
        P("ep", "rep", None, None, "opt"),
        P("ep", "rep", None, None, "opt"),
        P(),
        P("ep", None, None),
        P("ep", None, None),
        P("ep", None, None),
        P("ep", "rep", "opt"),
        P("ep", "rep", "opt"),
    )
    out_specs = (P("ep", "rep", "opt"), P("ep", "rep", "opt"), P("ep", None, "opt"))
    return jax.shard_map(shards, mesh=mesh, in_specs=in_specs, out_specs=out_specs, check_vma=False)
```

```python
import functools

import jax
import jax.numpy as jnp
from jax import lax
from jax.experimental import pallas as pl
from jax.experimental.pallas import tpu as pltpu
from jax.sharding import PartitionSpec as P

beta_one = 0.9
beta_two = 0.999
adam_step = 1000.0
adam_eps = 1e-08

MESH = pl.DeviceIdType.MESH
BF16 = jnp.bfloat16
F32 = jnp.float32

BLOCKS = 8
SUB = 16
RANK = 512
FEAT = 256
MODEL = 2048
FF = 768
OWN = 64

SLOTS = (
    (0, 0), (0, 1), (1, 0), (1, 1), (-1, 0), (-1, 1),
    (2, 0), (2, 1), (-2, 0), (-2, 1),
    (3, 0), (3, 1), (-3, 0), (-3, 1),
    (4, 0), (4, 1),
)
CHUNKS = ((0, 6), (6, 10), (10, 14), (14, 16))
PLACE = {q: (n, q - low) for n, (low, high) in enumerate(CHUNKS) for q in range(low, high)}
TOKEN_ORDER = ((2, 4, 3, 5, 1), (6, 8, 7, 9), (10, 12, 11, 13), (14, 15))
COT_FIRST = (10, 12, 11, 13, 6, 8, 7, 9, 2, 4, 3, 5, 1)
COT_LATER = (14, 15)
DIRECT = (1, 7, 2, 6)
REP_HOPS = (4, 3, 5, 2, 6, 1, 7)
SCHEDULE = (
    ("tokens", 0), ("tokens", 1),
    ("project", 0), ("hop", 0, 0), ("tokens", 2),
    ("project", 1), ("hop", 1, 0), ("hop", 0, 1), ("tokens", 3), ("hop", 0, 2), ("hop", 1, 1),
    ("project", 2), ("direct", 2), ("hop", 0, 3), ("hop", 1, 2),
    ("project", 3), ("direct", 3), ("cot",), ("hop", 1, 3), ("pass", 2), ("pass", 3),
    ("grad", 0), ("grad", 1), ("grad", 2), ("grad", 3),
)


class Transfers:
    def __init__(self):
        self.sends, self.arrivals = {}, {}

    def start(self, name, copy):
        copy.start()
        self.sends[name] = self.arrivals[name] = copy

    def sent(self, name):
        if name in self.sends:
            self.sends.pop(name).wait_send()

    def arrived(self, name):
        if name in self.arrivals:
            self.arrivals.pop(name).wait_recv()

    def finish(self):
        for name in list(self.arrivals):
            self.arrived(name)
        for name in list(self.sends):
            self.sent(name)


def adam(moment_first, moment_second, gradient):
    first_moment = beta_one * moment_first + (1.0 - beta_one) * gradient
    second_moment = beta_two * moment_second + (1.0 - beta_two) * gradient * gradient
    scaled_first = first_moment / (1.0 - beta_one**adam_step)
    scaled_second = second_moment / (1.0 - beta_two**adam_step)
    update = (-scaled_first / (jnp.sqrt(scaled_second) + adam_eps)).astype(BF16)
    return first_moment, second_moment, update


def rows_of(chunk):
    low, high = CHUNKS[chunk]
    return (high - low) * SUB


def kernel(
    dest_ref, tok_hbm, cot_hbm, gate_hbm, up_hbm, basis_hbm, m1_hbm, m2_hbm,
    gradient_out, update_out,
    gate_v, up_v, basis_v, cot_v, m1_v, m2_v, xtok, csend, tsend, hidden, grad, gsend, grecv, upd,
    crecv, trecv, proj,
    local_sem, xs, xr, cs, cr, ts, tr, ps, pr, gs, gr, us, ur,
):
    e = lax.axis_index("ep")
    r = lax.axis_index("rep")
    o = lax.axis_index("opt")
    z, c = lax.div(e, 2), lax.rem(e, 2)

    def ep_of(q):
        dz, dc = SLOTS[q]
        core = 1 - c if dc else c
        return lax.rem(z + (dz + 8), 8) * 2 + core

    def turn(axis_index, k):
        return lax.rem(axis_index + k, 8)

    own_features = pl.ds(pl.multiple_of(o * FEAT, FEAT), FEAT)
    loads = [
        pltpu.make_async_copy(cot_hbm, cot_v, local_sem.at[0]),
        pltpu.make_async_copy(tok_hbm.at[:, o], xtok.at[:, :, own_features], local_sem.at[1]),
        pltpu.make_async_copy(basis_hbm.at[0], basis_v, local_sem.at[2]),
        pltpu.make_async_copy(gate_hbm.at[0], gate_v, local_sem.at[3]),
        pltpu.make_async_copy(up_hbm.at[0], up_v, local_sem.at[4]),
        pltpu.make_async_copy(m1_hbm.at[0], m1_v, local_sem.at[5]),
        pltpu.make_async_copy(m2_hbm.at[0], m2_v, local_sem.at[6]),
    ]
    for load in loads:
        load.start()

    barrier = pltpu.get_barrier_semaphore()
    for k in range(1, 8):
        pl.semaphore_signal(barrier, inc=1, device_id={"opt": turn(o, k)}, device_id_type=MESH)
    for k in REP_HOPS:
        pl.semaphore_signal(barrier, inc=1, device_id={"rep": turn(r, k)}, device_id_type=MESH)
    for q in range(1, 16):
        pl.semaphore_signal(barrier, inc=1, device_id={"ep": ep_of(q)}, device_id_type=MESH)
    pl.semaphore_wait(barrier, 22 + len(REP_HOPS))

    def x_copy(k):
        return pltpu.make_async_remote_copy(
            src_ref=tok_hbm.at[:, turn(o, k)],
            dst_ref=xtok.at[:, :, own_features],
            send_sem=xs.at[k],
            recv_sem=xr.at[k],
            device_id={"opt": turn(o, k)},
            device_id_type=MESH,
        )

    moving = Transfers()
    for k in range(1, 8):
        moving.start(("x", k), x_copy(k))

    dest = [dest_ref[r, b, e] for b in range(BLOCKS)]

    def block_for(q):
        target = ep_of(q)
        index, found = jnp.int32(0), jnp.int32(0)
        for b in range(BLOCKS):
            hit = dest[b] == target
            index = jnp.where(hit, b, index)
            found = jnp.where(hit, 1, found)
        return index, found

    def cot_copy(q):
        return pltpu.make_async_remote_copy(
            src_ref=csend.at[q],
            dst_ref=crecv[PLACE[q][0]].at[:, PLACE[q][1]],
            send_sem=cs.at[q],
            recv_sem=cr.at[q],
            device_id={"ep": ep_of(q)},
            device_id_type=MESH,
        )

    def token_copy(q):
        return pltpu.make_async_remote_copy(
            src_ref=tsend.at[q],
            dst_ref=trecv[PLACE[q][0]].at[PLACE[q][1]],
            send_sem=ts.at[q],
            recv_sem=tr.at[q],
            device_id={"ep": ep_of(q)},
            device_id_type=MESH,
        )

    def send_cot(q):
        index, _ = block_for(q)
        csend[q] = cot_v[index]
        moving.start(("cot", q), cot_copy(q))

    def token_slot(q):
        index, found = block_for(q)
        rows = xtok[index]
        return jnp.where(found > 0, rows, jnp.zeros_like(rows))

    loads[0].wait()
    for q in COT_FIRST:
        send_cot(q)
    crecv[0][:, 0] = cot_v[block_for(0)[0]]

    loads[1].wait()
    for k in range(1, 8):
        moving.arrived(("x", k))

    def send_tokens(chunk):
        for q in TOKEN_ORDER[chunk]:
            tsend[q] = token_slot(q)
            moving.start(("token", q), token_copy(q))

    trecv[0][0] = token_slot(0)

    def direct(chunk, k):
        return pltpu.make_async_remote_copy(
            src_ref=proj[chunk].at[o],
            dst_ref=proj[chunk].at[o],
            send_sem=ps.at[chunk, k],
            recv_sem=pr.at[chunk, k],
            device_id={"opt": turn(o, k)},
            device_id_type=MESH,
        )

    def forwards(chunk):
        half = rows_of(chunk) // 2
        moves = (
            (turn(o, 6), 0, 2 * half, 1, 3),
            (turn(o, 2), 0, 2 * half, 7, 5),
            (turn(o, 6), 0, half, 2, 4),
            (turn(o, 2), half, half, 6, 0),
        )
        return [
            (
                sem,
                pltpu.make_async_remote_copy(
                    src_ref=proj[chunk].at[source, pl.ds(low, size)],
                    dst_ref=proj[chunk].at[source, pl.ds(low, size)],
                    send_sem=ps.at[chunk, sem],
                    recv_sem=pr.at[chunk, sem],
                    device_id={"opt": turn(o, k)},
                    device_id_type=MESH,
                ),
            )
            for source, low, size, k, sem in moves
        ]

    waiting = loads[2:5]

    def weights():
        while waiting:
            waiting.pop(0).wait()

    def project(chunk):
        weights()
        for q in range(*CHUNKS[chunk]):
            moving.arrived(("token", q))
        rows = trecv[chunk][...].reshape(rows_of(chunk), MODEL)
        local = pl.ds(0, rows_of(chunk))
        for part in range(3):
            columns = pl.ds(part * 256, 256)
            gate = jnp.dot(rows, gate_v[:, columns], preferred_element_type=F32)
            up = jnp.dot(rows, up_v[:, columns], preferred_element_type=F32)
            hidden[local, columns] = (gate / (1.0 + jnp.exp(-gate)) * up).astype(BF16)
        projected = jnp.dot(hidden[local, :], basis_v[...], preferred_element_type=F32)
        proj[chunk][o] = projected.astype(BF16)

    def send_direct(chunk):
        for k in DIRECT:
            moving.start(("proj", chunk, k), direct(chunk, k))

    def hop(chunk, stage):
        size = rows_of(chunk)
        half = size // 2 if stage == 3 else size
        moving.arrived(("proj", chunk, stage))
        moving.arrived(("proj", chunk, 8 - stage))
        for source, low, k, sem in (
            (turn(o, 8 - stage), 0, 1, stage + 1),
            (turn(o, stage), size - half, 7, 0 if stage == 3 else 7 - stage),
        ):
            piece = proj[chunk].at[source, pl.ds(low, half)]
            copy = pltpu.make_async_remote_copy(
                src_ref=piece,
                dst_ref=piece,
                send_sem=ps.at[chunk, sem],
                recv_sem=pr.at[chunk, sem],
                device_id={"opt": turn(o, k)},
                device_id_type=MESH,
            )
            moving.start(("proj", chunk, sem), copy)

    def pass_on(chunk):
        moving.arrived(("proj", chunk, 2))
        moving.arrived(("proj", chunk, 6))
        for sem, copy in forwards(chunk):
            moving.start(("proj", chunk, sem), copy)

    def contract(chunk):
        for q in range(*CHUNKS[chunk]):
            moving.arrived(("cot", q))
        for k in range(8):
            moving.arrived(("proj", chunk, k))
        term = lax.dot_general(
            proj[chunk][...].reshape(8 * rows_of(chunk), RANK),
            crecv[chunk][...].reshape(8 * rows_of(chunk), FEAT),
            (((0,), (0,)), ((), ())),
            preferred_element_type=F32,
        )
        grad[...] = term if chunk == 0 else grad[...] + term

    def send_cots():
        for q in COT_LATER:
            send_cot(q)

    run = {
        "tokens": send_tokens,
        "project": project,
        "hop": hop,
        "direct": send_direct,
        "pass": pass_on,
        "cot": send_cots,
        "grad": contract,
    }
    for step, *where in SCHEDULE:
        run[step](*where)
    weights()
    gsend[...] = grad[...].astype(BF16)

    def grad_copy(k):
        rows = pl.ds(pl.multiple_of(turn(r, k) * OWN, OWN), OWN)
        return pltpu.make_async_remote_copy(
            src_ref=gsend.at[rows],
            dst_ref=grecv.at[k],
            send_sem=gs.at[k],
            recv_sem=gr.at[k],
            device_id={"rep": turn(r, k)},
            device_id_type=MESH,
        )

    for k in REP_HOPS:
        moving.start(("grad", k), grad_copy(k))
    own_rows = pl.ds(pl.multiple_of(r * OWN, OWN), OWN)
    gradient = grad[own_rows, :]
    loads[5].wait()
    loads[6].wait()
    for k in REP_HOPS:
        moving.arrived(("grad", k))
    for k in REP_HOPS:
        gradient += grecv[k].astype(F32)
    gradient_out[...] = gradient
    upd[own_rows, :] = adam(m1_v[...], m2_v[...], gradient)[2]

    def update_copy(k):
        return pltpu.make_async_remote_copy(
            src_ref=upd.at[own_rows],
            dst_ref=upd.at[own_rows],
            send_sem=us.at[k],
            recv_sem=ur.at[k],
            device_id={"rep": turn(r, k)},
            device_id_type=MESH,
        )

    for k in REP_HOPS:
        moving.start(("update", k), update_copy(k))
    moving.finish()
    update_out[...] = upd[...]


def finish(gradient_ref, update_ref, basis_ref, m1_ref, m2_ref, m1_out, m2_out, delta_out):
    first_moment, second_moment, _ = adam(m1_ref[0], m2_ref[0], gradient_ref[...])
    m1_out[0] = first_moment
    m2_out[0] = second_moment
    delta_out[0] = jnp.dot(basis_ref[0], update_ref[...], preferred_element_type=F32).astype(BF16)


def shards(
    incoming_tokens,
    cotangent,
    block_dest,
    gate_weight,
    up_weight,
    basis,
    moment_first,
    moment_second,
):
    tokens = incoming_tokens.reshape(BLOCKS, 8, SUB, FEAT)
    cot = cotangent.reshape(BLOCKS, 8, SUB, FEAT)
    hbm = pl.BlockSpec(memory_space=pl.ANY)
    vmem = pl.BlockSpec(memory_space=pltpu.VMEM)
    dma = pltpu.SemaphoreType.DMA
    gradient, update = pl.pallas_call(
        kernel,
        out_shape=(
            jax.ShapeDtypeStruct((OWN, FEAT), F32),
            jax.ShapeDtypeStruct((RANK, FEAT), BF16),
        ),
        in_specs=[pl.BlockSpec(memory_space=pltpu.SMEM)] + [hbm] * 7,
        out_specs=(vmem, vmem),
        scratch_shapes=[
            pltpu.VMEM((MODEL, FF), BF16),
            pltpu.VMEM((MODEL, FF), BF16),
            pltpu.VMEM((FF, RANK), BF16),
            pltpu.VMEM((BLOCKS, 8, SUB, FEAT), BF16),
            pltpu.VMEM((OWN, FEAT), F32),
            pltpu.VMEM((OWN, FEAT), F32),
            pltpu.VMEM((BLOCKS, SUB, MODEL), BF16),
            pltpu.VMEM((16, 8, SUB, FEAT), BF16),
            pltpu.VMEM((16, SUB, MODEL), BF16),
            pltpu.VMEM((rows_of(0), FF), BF16),
            pltpu.VMEM((RANK, FEAT), F32),
            pltpu.VMEM((RANK, FEAT), BF16),
            pltpu.VMEM((8, OWN, FEAT), BF16),
            pltpu.VMEM((RANK, FEAT), BF16),
            [pltpu.VMEM((8, high - low, SUB, FEAT), BF16) for low, high in CHUNKS],
            [pltpu.VMEM((high - low, SUB, MODEL), BF16) for low, high in CHUNKS],
            [pltpu.VMEM((8, (high - low) * SUB, RANK), BF16) for low, high in CHUNKS],
            dma((7,)),
            dma((8,)), dma((8,)),
            dma((16,)), dma((16,)),
            dma((16,)), dma((16,)),
            dma((len(CHUNKS), 8)), dma((len(CHUNKS), 8)),
            dma((8,)), dma((8,)),
            dma((8,)), dma((8,)),
        ],
        compiler_params=pltpu.CompilerParams(
            collective_id=0, has_side_effects=True, vmem_limit_bytes=63 * 1024 * 1024
        ),
    )(
        jnp.transpose(block_dest, (1, 2, 0)),
        tokens,
        cot,
        gate_weight,
        up_weight,
        basis,
        moment_first,
        moment_second,
    )
    return pl.pallas_call(
        finish,
        out_shape=(
            jax.ShapeDtypeStruct((1, OWN, FEAT), F32),
            jax.ShapeDtypeStruct((1, OWN, FEAT), F32),
            jax.ShapeDtypeStruct((1, FF, FEAT), BF16),
        ),
        in_specs=[vmem] * 5,
        out_specs=(vmem, vmem, vmem),
        cost_estimate=pl.CostEstimate(flops=2 * FF * RANK * FEAT, bytes_accessed=2**21, transcendentals=0),
    )(gradient, update, basis, moment_first, moment_second)


def solution(mesh):
    in_specs = (
        P("ep", "rep", None, None, "opt"),
        P("ep", "rep", None, None, "opt"),
        P(),
        P("ep", None, None),
        P("ep", None, None),
        P("ep", None, None),
        P("ep", "rep", "opt"),
        P("ep", "rep", "opt"),
    )
    out_specs = (P("ep", "rep", "opt"), P("ep", "rep", "opt"), P("ep", None, "opt"))
    return jax.shard_map(shards, mesh=mesh, in_specs=in_specs, out_specs=out_specs, check_vma=False)
```

```python
import functools

import jax
import jax.numpy as jnp
from jax import lax
from jax.experimental import pallas as pl
from jax.experimental.pallas import tpu as pltpu
from jax.sharding import PartitionSpec as P

beta_one = 0.9
beta_two = 0.999
adam_step = 1000.0
adam_eps = 1e-08

MESH = pl.DeviceIdType.MESH
BF16 = jnp.bfloat16
F32 = jnp.float32

BLOCKS = 8
SUB = 16
RANK = 512
FEAT = 256
MODEL = 2048
FF = 768
OWN = 64
PARTS = 2
PART = OWN // PARTS

SLOTS = (
    (0, 0), (0, 1), (1, 0), (1, 1), (-1, 0), (-1, 1),
    (2, 0), (2, 1), (-2, 0), (-2, 1),
    (3, 0), (3, 1), (-3, 0), (-3, 1),
    (4, 0), (4, 1),
)
CHUNKS = ((0, 6), (6, 10), (10, 14), (14, 16))
PLACE = {q: (n, q - low) for n, (low, high) in enumerate(CHUNKS) for q in range(low, high)}
TOKEN_ORDER = ((2, 4, 3, 5, 1), (6, 8, 7, 9), (10, 12, 11, 13), (14, 15))
COT_FIRST = (10, 12, 11, 13, 6, 8, 7, 9, 2, 4, 3, 5, 1)
COT_LATER = (14, 15)
DIRECT = (1, 7, 2, 6)
REP_HOPS = (4, 3, 5, 2, 6, 1, 7)
SCHEDULE = (
    ("tokens", 0), ("tokens", 1),
    ("project", 0), ("hop", 0, 0), ("tokens", 2), ("hop", 0, 1),
    ("project", 1), ("hop", 1, 0), ("tokens", 3), ("hop", 0, 2), ("hop", 1, 1),
    ("project", 2), ("direct", 2), ("hop", 0, 3), ("hop", 1, 2),
    ("project", 3), ("direct", 3), ("cot",), ("hop", 1, 3), ("pass", 2), ("pass", 3),
    ("grad", 0), ("grad", 1), ("grad", 2), ("grad", 3),
)


class Transfers:
    def __init__(self):
        self.sends, self.arrivals = {}, {}

    def start(self, name, copy):
        copy.start()
        self.sends[name] = self.arrivals[name] = copy

    def sent(self, name):
        if name in self.sends:
            self.sends.pop(name).wait_send()

    def arrived(self, name):
        if name in self.arrivals:
            self.arrivals.pop(name).wait_recv()

    def finish(self):
        for name in list(self.arrivals):
            self.arrived(name)
        for name in list(self.sends):
            self.sent(name)


def adam(moment_first, moment_second, gradient):
    first_moment = beta_one * moment_first + (1.0 - beta_one) * gradient
    second_moment = beta_two * moment_second + (1.0 - beta_two) * gradient * gradient
    scaled_first = first_moment / (1.0 - beta_one**adam_step)
    scaled_second = second_moment / (1.0 - beta_two**adam_step)
    update = (-scaled_first / (jnp.sqrt(scaled_second) + adam_eps)).astype(BF16)
    return first_moment, second_moment, update


def rows_of(chunk):
    low, high = CHUNKS[chunk]
    return (high - low) * SUB


def kernel(
    dest_ref, tok_hbm, cot_hbm, gate_hbm, up_hbm, basis_hbm, m1_hbm, m2_hbm,
    gradient_out, update_out,
    gate_v, up_v, basis_v, cot_v, m1_v, m2_v, xtok, csend, tsend, hidden, grad, gsend, grecv, upd,
    crecv, trecv, proj,
    local_sem, xs, xr, cs, cr, ts, tr, ps, pr, gs, gr, us, ur,
):
    e = lax.axis_index("ep")
    r = lax.axis_index("rep")
    o = lax.axis_index("opt")
    z, c = lax.div(e, 2), lax.rem(e, 2)

    def ep_of(q):
        dz, dc = SLOTS[q]
        core = 1 - c if dc else c
        return lax.rem(z + (dz + 8), 8) * 2 + core

    def turn(axis_index, k):
        return lax.rem(axis_index + k, 8)

    own_features = pl.ds(pl.multiple_of(o * FEAT, FEAT), FEAT)
    loads = [
        pltpu.make_async_copy(cot_hbm, cot_v, local_sem.at[0]),
        pltpu.make_async_copy(tok_hbm.at[:, o], xtok.at[:, :, own_features], local_sem.at[1]),
        pltpu.make_async_copy(basis_hbm.at[0], basis_v, local_sem.at[2]),
        pltpu.make_async_copy(gate_hbm.at[0], gate_v, local_sem.at[3]),
        pltpu.make_async_copy(up_hbm.at[0], up_v, local_sem.at[4]),
        pltpu.make_async_copy(m1_hbm.at[0], m1_v, local_sem.at[5]),
        pltpu.make_async_copy(m2_hbm.at[0], m2_v, local_sem.at[6]),
    ]
    for load in loads:
        load.start()

    barrier = pltpu.get_barrier_semaphore()
    for k in range(1, 8):
        pl.semaphore_signal(barrier, inc=1, device_id={"opt": turn(o, k)}, device_id_type=MESH)
    for k in REP_HOPS:
        pl.semaphore_signal(barrier, inc=1, device_id={"rep": turn(r, k)}, device_id_type=MESH)
    for q in range(1, 16):
        pl.semaphore_signal(barrier, inc=1, device_id={"ep": ep_of(q)}, device_id_type=MESH)
    pl.semaphore_wait(barrier, 22 + len(REP_HOPS))

    def x_copy(k):
        return pltpu.make_async_remote_copy(
            src_ref=tok_hbm.at[:, turn(o, k)],
            dst_ref=xtok.at[:, :, own_features],
            send_sem=xs.at[k],
            recv_sem=xr.at[k],
            device_id={"opt": turn(o, k)},
            device_id_type=MESH,
        )

    moving = Transfers()
    for k in range(1, 8):
        moving.start(("x", k), x_copy(k))

    dest = [dest_ref[r, b, e] for b in range(BLOCKS)]

    def block_for(q):
        target = ep_of(q)
        index, found = jnp.int32(0), jnp.int32(0)
        for b in range(BLOCKS):
            hit = dest[b] == target
            index = jnp.where(hit, b, index)
            found = jnp.where(hit, 1, found)
        return index, found

    def cot_copy(q):
        return pltpu.make_async_remote_copy(
            src_ref=csend.at[q],
            dst_ref=crecv[PLACE[q][0]].at[:, PLACE[q][1]],
            send_sem=cs.at[q],
            recv_sem=cr.at[q],
            device_id={"ep": ep_of(q)},
            device_id_type=MESH,
        )

    def token_copy(q):
        return pltpu.make_async_remote_copy(
            src_ref=tsend.at[q],
            dst_ref=trecv[PLACE[q][0]].at[PLACE[q][1]],
            send_sem=ts.at[q],
            recv_sem=tr.at[q],
            device_id={"ep": ep_of(q)},
            device_id_type=MESH,
        )

    def send_cot(q):
        index, _ = block_for(q)
        csend[q] = cot_v[index]
        moving.start(("cot", q), cot_copy(q))

    def token_slot(q):
        index, found = block_for(q)
        rows = xtok[index]
        return jnp.where(found > 0, rows, jnp.zeros_like(rows))

    loads[0].wait()
    for q in COT_FIRST:
        send_cot(q)
    crecv[0][:, 0] = cot_v[block_for(0)[0]]

    loads[1].wait()
    for k in range(1, 8):
        moving.arrived(("x", k))

    def send_tokens(chunk):
        for q in TOKEN_ORDER[chunk]:
            tsend[q] = token_slot(q)
            moving.start(("token", q), token_copy(q))

    trecv[0][0] = token_slot(0)

    def direct(chunk, k):
        return pltpu.make_async_remote_copy(
            src_ref=proj[chunk].at[o],
            dst_ref=proj[chunk].at[o],
            send_sem=ps.at[chunk, k],
            recv_sem=pr.at[chunk, k],
            device_id={"opt": turn(o, k)},
            device_id_type=MESH,
        )

    def forwards(chunk):
        half = rows_of(chunk) // 2
        moves = (
            (turn(o, 6), 0, 2 * half, 1, 3),
            (turn(o, 2), 0, 2 * half, 7, 5),
            (turn(o, 6), 0, half, 2, 4),
            (turn(o, 2), half, half, 6, 0),
        )
        return [
            (
                sem,
                pltpu.make_async_remote_copy(
                    src_ref=proj[chunk].at[source, pl.ds(low, size)],
                    dst_ref=proj[chunk].at[source, pl.ds(low, size)],
                    send_sem=ps.at[chunk, sem],
                    recv_sem=pr.at[chunk, sem],
                    device_id={"opt": turn(o, k)},
                    device_id_type=MESH,
                ),
            )
            for source, low, size, k, sem in moves
        ]

    waiting = loads[2:5]

    def weights():
        while waiting:
            waiting.pop(0).wait()

    def project(chunk):
        weights()
        for q in range(*CHUNKS[chunk]):
            moving.arrived(("token", q))
        rows = trecv[chunk][...].reshape(rows_of(chunk), MODEL)
        local = pl.ds(0, rows_of(chunk))
        for part in range(3):
            columns = pl.ds(part * 256, 256)
            gate = jnp.dot(rows, gate_v[:, columns], preferred_element_type=F32)
            up = jnp.dot(rows, up_v[:, columns], preferred_element_type=F32)
            hidden[local, columns] = (gate / (1.0 + jnp.exp(-gate)) * up).astype(BF16)
        projected = jnp.dot(hidden[local, :], basis_v[...], preferred_element_type=F32)
        proj[chunk][o] = projected.astype(BF16)

    def send_direct(chunk):
        for k in DIRECT:
            moving.start(("proj", chunk, k), direct(chunk, k))

    def hop(chunk, stage):
        size = rows_of(chunk)
        half = size // 2 if stage == 3 else size
        moving.arrived(("proj", chunk, stage))
        moving.arrived(("proj", chunk, 8 - stage))
        for source, low, k, sem in (
            (turn(o, 8 - stage), 0, 1, stage + 1),
            (turn(o, stage), size - half, 7, 0 if stage == 3 else 7 - stage),
        ):
            piece = proj[chunk].at[source, pl.ds(low, half)]
            copy = pltpu.make_async_remote_copy(
                src_ref=piece,
                dst_ref=piece,
                send_sem=ps.at[chunk, sem],
                recv_sem=pr.at[chunk, sem],
                device_id={"opt": turn(o, k)},
                device_id_type=MESH,
            )
            moving.start(("proj", chunk, sem), copy)

    def pass_on(chunk):
        moving.arrived(("proj", chunk, 2))
        moving.arrived(("proj", chunk, 6))
        for sem, copy in forwards(chunk):
            moving.start(("proj", chunk, sem), copy)

    def contract(chunk):
        for q in range(*CHUNKS[chunk]):
            moving.arrived(("cot", q))
        for k in range(8):
            moving.arrived(("proj", chunk, k))
        term = lax.dot_general(
            proj[chunk][...].reshape(8 * rows_of(chunk), RANK),
            crecv[chunk][...].reshape(8 * rows_of(chunk), FEAT),
            (((0,), (0,)), ((), ())),
            preferred_element_type=F32,
        )
        grad[...] = term if chunk == 0 else grad[...] + term

    def send_cots():
        for q in COT_LATER:
            send_cot(q)

    run = {
        "tokens": send_tokens,
        "project": project,
        "hop": hop,
        "direct": send_direct,
        "pass": pass_on,
        "cot": send_cots,
        "grad": contract,
    }
    for step, *where in SCHEDULE:
        run[step](*where)
    weights()
    gsend[...] = grad[...].astype(BF16)

    def part_rows(owner, part):
        return pl.ds(pl.multiple_of(owner * OWN + part * PART, PART), PART)

    def grad_copy(k, part):
        return pltpu.make_async_remote_copy(
            src_ref=gsend.at[part_rows(turn(r, k), part)],
            dst_ref=grecv.at[k, pl.ds(part * PART, PART)],
            send_sem=gs.at[part, k],
            recv_sem=gr.at[part, k],
            device_id={"rep": turn(r, k)},
            device_id_type=MESH,
        )

    def update_copy(k, part):
        rows = part_rows(r, part)
        return pltpu.make_async_remote_copy(
            src_ref=upd.at[rows],
            dst_ref=upd.at[rows],
            send_sem=us.at[part, k],
            recv_sem=ur.at[part, k],
            device_id={"rep": turn(r, k)},
            device_id_type=MESH,
        )

    for part in range(PARTS):
        for k in REP_HOPS:
            moving.start(("grad", k, part), grad_copy(k, part))
    loads[5].wait()
    loads[6].wait()
    for part in range(PARTS):
        local = pl.ds(part * PART, PART)
        rows = part_rows(r, part)
        gradient = grad[rows, :]
        for k in REP_HOPS:
            moving.arrived(("grad", k, part))
        for k in REP_HOPS:
            gradient += grecv[k, local].astype(F32)
        gradient_out[local, :] = gradient
        upd[rows, :] = adam(m1_v[local, :], m2_v[local, :], gradient)[2]
        for k in REP_HOPS:
            moving.start(("update", k, part), update_copy(k, part))
    moving.finish()
    update_out[...] = upd[...]


def finish(gradient_ref, update_ref, basis_ref, m1_ref, m2_ref, m1_out, m2_out, delta_out):
    first_moment, second_moment, _ = adam(m1_ref[0], m2_ref[0], gradient_ref[...])
    m1_out[0] = first_moment
    m2_out[0] = second_moment
    delta_out[0] = jnp.dot(basis_ref[0], update_ref[...], preferred_element_type=F32).astype(BF16)


def shards(
    incoming_tokens,
    cotangent,
    block_dest,
    gate_weight,
    up_weight,
    basis,
    moment_first,
    moment_second,
):
    tokens = incoming_tokens.reshape(BLOCKS, 8, SUB, FEAT)
    cot = cotangent.reshape(BLOCKS, 8, SUB, FEAT)
    hbm = pl.BlockSpec(memory_space=pl.ANY)
    vmem = pl.BlockSpec(memory_space=pltpu.VMEM)
    dma = pltpu.SemaphoreType.DMA
    gradient, update = pl.pallas_call(
        kernel,
        out_shape=(
            jax.ShapeDtypeStruct((OWN, FEAT), F32),
            jax.ShapeDtypeStruct((RANK, FEAT), BF16),
        ),
        in_specs=[pl.BlockSpec(memory_space=pltpu.SMEM)] + [hbm] * 7,
        out_specs=(vmem, vmem),
        scratch_shapes=[
            pltpu.VMEM((MODEL, FF), BF16),
            pltpu.VMEM((MODEL, FF), BF16),
            pltpu.VMEM((FF, RANK), BF16),
            pltpu.VMEM((BLOCKS, 8, SUB, FEAT), BF16),
            pltpu.VMEM((OWN, FEAT), F32),
            pltpu.VMEM((OWN, FEAT), F32),
            pltpu.VMEM((BLOCKS, SUB, MODEL), BF16),
            pltpu.VMEM((16, 8, SUB, FEAT), BF16),
            pltpu.VMEM((16, SUB, MODEL), BF16),
            pltpu.VMEM((rows_of(0), FF), BF16),
            pltpu.VMEM((RANK, FEAT), F32),
            pltpu.VMEM((RANK, FEAT), BF16),
            pltpu.VMEM((8, OWN, FEAT), BF16),
            pltpu.VMEM((RANK, FEAT), BF16),
            [pltpu.VMEM((8, high - low, SUB, FEAT), BF16) for low, high in CHUNKS],
            [pltpu.VMEM((high - low, SUB, MODEL), BF16) for low, high in CHUNKS],
            [pltpu.VMEM((8, (high - low) * SUB, RANK), BF16) for low, high in CHUNKS],
            dma((7,)),
            dma((8,)), dma((8,)),
            dma((16,)), dma((16,)),
            dma((16,)), dma((16,)),
            dma((len(CHUNKS), 8)), dma((len(CHUNKS), 8)),
            dma((PARTS, 8)), dma((PARTS, 8)),
            dma((PARTS, 8)), dma((PARTS, 8)),
        ],
        compiler_params=pltpu.CompilerParams(
            collective_id=0, has_side_effects=True, vmem_limit_bytes=63 * 1024 * 1024
        ),
    )(
        jnp.transpose(block_dest, (1, 2, 0)),
        tokens,
        cot,
        gate_weight,
        up_weight,
        basis,
        moment_first,
        moment_second,
    )
    return pl.pallas_call(
        finish,
        out_shape=(
            jax.ShapeDtypeStruct((1, OWN, FEAT), F32),
            jax.ShapeDtypeStruct((1, OWN, FEAT), F32),
            jax.ShapeDtypeStruct((1, FF, FEAT), BF16),
        ),
        in_specs=[vmem] * 5,
        out_specs=(vmem, vmem, vmem),
        cost_estimate=pl.CostEstimate(flops=2 * FF * RANK * FEAT, bytes_accessed=2**21, transcendentals=0),
    )(gradient, update, basis, moment_first, moment_second)


def solution(mesh):
    in_specs = (
        P("ep", "rep", None, None, "opt"),
        P("ep", "rep", None, None, "opt"),
        P(),
        P("ep", None, None),
        P("ep", None, None),
        P("ep", None, None),
        P("ep", "rep", "opt"),
        P("ep", "rep", "opt"),
    )
    out_specs = (P("ep", "rep", "opt"), P("ep", "rep", "opt"), P("ep", None, "opt"))
    return jax.shard_map(shards, mesh=mesh, in_specs=in_specs, out_specs=out_specs, check_vma=False)
```

```python
import functools

import jax
import jax.numpy as jnp
from jax import lax
from jax.experimental import pallas as pl
from jax.experimental.pallas import tpu as pltpu
from jax.sharding import PartitionSpec as P

beta_one = 0.9
beta_two = 0.999
adam_step = 1000.0
adam_eps = 1e-08

MESH = pl.DeviceIdType.MESH
BF16 = jnp.bfloat16
F32 = jnp.float32

BLOCKS = 8
SUB = 16
RANK = 512
FEAT = 256
MODEL = 2048
FF = 768
OWN = 64
PARTS = 4
PART = OWN // PARTS

SLOTS = (
    (0, 0), (0, 1), (1, 0), (1, 1), (-1, 0), (-1, 1),
    (2, 0), (2, 1), (-2, 0), (-2, 1),
    (3, 0), (3, 1), (-3, 0), (-3, 1),
    (4, 0), (4, 1),
)
CHUNKS = ((0, 6), (6, 10), (10, 14), (14, 16))
PLACE = {q: (n, q - low) for n, (low, high) in enumerate(CHUNKS) for q in range(low, high)}
TOKEN_ORDER = ((2, 4, 3, 5, 1), (6, 8, 7, 9), (10, 12, 11, 13), (14, 15))
COT_FIRST = (10, 12, 11, 13, 6, 8, 7, 9, 2, 4, 3, 5, 1)
COT_LATER = (14, 15)
DIRECT = (1, 7, 2, 6)
REP_HOPS = (4, 3, 5, 2, 6, 1, 7)
SCHEDULE = (
    ("tokens", 0), ("tokens", 1),
    ("project", 0), ("hop", 0, 0), ("tokens", 2), ("hop", 0, 1),
    ("project", 1), ("hop", 1, 0), ("tokens", 3), ("hop", 0, 2), ("hop", 1, 1),
    ("project", 2), ("direct", 2), ("hop", 0, 3), ("hop", 1, 2),
    ("project", 3), ("direct", 3), ("cot",), ("hop", 1, 3), ("pass", 2), ("pass", 3),
    ("grad", 0), ("grad", 1), ("grad", 2), ("grad", 3),
)


class Transfers:
    def __init__(self):
        self.sends, self.arrivals = {}, {}

    def start(self, name, copy):
        copy.start()
        self.sends[name] = self.arrivals[name] = copy

    def sent(self, name):
        if name in self.sends:
            self.sends.pop(name).wait_send()

    def arrived(self, name):
        if name in self.arrivals:
            self.arrivals.pop(name).wait_recv()

    def finish(self):
        for name in list(self.arrivals):
            self.arrived(name)
        for name in list(self.sends):
            self.sent(name)


def adam(moment_first, moment_second, gradient):
    first_moment = beta_one * moment_first + (1.0 - beta_one) * gradient
    second_moment = beta_two * moment_second + (1.0 - beta_two) * gradient * gradient
    scaled_first = first_moment / (1.0 - beta_one**adam_step)
    scaled_second = second_moment / (1.0 - beta_two**adam_step)
    update = (-scaled_first / (jnp.sqrt(scaled_second) + adam_eps)).astype(BF16)
    return first_moment, second_moment, update


def rows_of(chunk):
    low, high = CHUNKS[chunk]
    return (high - low) * SUB


def kernel(
    dest_ref, tok_hbm, cot_hbm, gate_hbm, up_hbm, basis_hbm, m1_hbm, m2_hbm,
    gradient_out, update_out,
    gate_v, up_v, basis_v, cot_v, m1_v, m2_v, xtok, csend, tsend, hidden, grad, gsend, grecv, upd,
    crecv, trecv, proj,
    local_sem, xs, xr, cs, cr, ts, tr, ps, pr, gs, gr, us, ur,
):
    e = lax.axis_index("ep")
    r = lax.axis_index("rep")
    o = lax.axis_index("opt")
    z, c = lax.div(e, 2), lax.rem(e, 2)

    def ep_of(q):
        dz, dc = SLOTS[q]
        core = 1 - c if dc else c
        return lax.rem(z + (dz + 8), 8) * 2 + core

    def turn(axis_index, k):
        return lax.rem(axis_index + k, 8)

    own_features = pl.ds(pl.multiple_of(o * FEAT, FEAT), FEAT)
    loads = [
        pltpu.make_async_copy(cot_hbm, cot_v, local_sem.at[0]),
        pltpu.make_async_copy(tok_hbm.at[:, o], xtok.at[:, :, own_features], local_sem.at[1]),
        pltpu.make_async_copy(basis_hbm.at[0], basis_v, local_sem.at[2]),
        pltpu.make_async_copy(gate_hbm.at[0], gate_v, local_sem.at[3]),
        pltpu.make_async_copy(up_hbm.at[0], up_v, local_sem.at[4]),
        pltpu.make_async_copy(m1_hbm.at[0], m1_v, local_sem.at[5]),
        pltpu.make_async_copy(m2_hbm.at[0], m2_v, local_sem.at[6]),
    ]
    for load in loads:
        load.start()

    barrier = pltpu.get_barrier_semaphore()
    for k in range(1, 8):
        pl.semaphore_signal(barrier, inc=1, device_id={"opt": turn(o, k)}, device_id_type=MESH)
    for k in REP_HOPS:
        pl.semaphore_signal(barrier, inc=1, device_id={"rep": turn(r, k)}, device_id_type=MESH)
    for q in range(1, 16):
        pl.semaphore_signal(barrier, inc=1, device_id={"ep": ep_of(q)}, device_id_type=MESH)
    pl.semaphore_wait(barrier, 22 + len(REP_HOPS))

    def x_copy(k):
        return pltpu.make_async_remote_copy(
            src_ref=tok_hbm.at[:, turn(o, k)],
            dst_ref=xtok.at[:, :, own_features],
            send_sem=xs.at[k],
            recv_sem=xr.at[k],
            device_id={"opt": turn(o, k)},
            device_id_type=MESH,
        )

    moving = Transfers()
    for k in range(1, 8):
        moving.start(("x", k), x_copy(k))

    dest = [dest_ref[r, b, e] for b in range(BLOCKS)]

    def block_for(q):
        target = ep_of(q)
        index, found = jnp.int32(0), jnp.int32(0)
        for b in range(BLOCKS):
            hit = dest[b] == target
            index = jnp.where(hit, b, index)
            found = jnp.where(hit, 1, found)
        return index, found

    def cot_copy(q):
        return pltpu.make_async_remote_copy(
            src_ref=csend.at[q],
            dst_ref=crecv[PLACE[q][0]].at[:, PLACE[q][1]],
            send_sem=cs.at[q],
            recv_sem=cr.at[q],
            device_id={"ep": ep_of(q)},
            device_id_type=MESH,
        )

    def token_copy(q):
        return pltpu.make_async_remote_copy(
            src_ref=tsend.at[q],
            dst_ref=trecv[PLACE[q][0]].at[PLACE[q][1]],
            send_sem=ts.at[q],
            recv_sem=tr.at[q],
            device_id={"ep": ep_of(q)},
            device_id_type=MESH,
        )

    def send_cot(q):
        index, _ = block_for(q)
        csend[q] = cot_v[index]
        moving.start(("cot", q), cot_copy(q))

    def token_slot(q):
        index, found = block_for(q)
        rows = xtok[index]
        return jnp.where(found > 0, rows, jnp.zeros_like(rows))

    loads[0].wait()
    for q in COT_FIRST:
        send_cot(q)
    crecv[0][:, 0] = cot_v[block_for(0)[0]]

    loads[1].wait()
    for k in range(1, 8):
        moving.arrived(("x", k))

    def send_tokens(chunk):
        for q in TOKEN_ORDER[chunk]:
            tsend[q] = token_slot(q)
            moving.start(("token", q), token_copy(q))

    trecv[0][0] = token_slot(0)

    def direct(chunk, k):
        return pltpu.make_async_remote_copy(
            src_ref=proj[chunk].at[o],
            dst_ref=proj[chunk].at[o],
            send_sem=ps.at[chunk, k],
            recv_sem=pr.at[chunk, k],
            device_id={"opt": turn(o, k)},
            device_id_type=MESH,
        )

    def forwards(chunk):
        half = rows_of(chunk) // 2
        moves = (
            (turn(o, 6), 0, 2 * half, 1, 3),
            (turn(o, 2), 0, 2 * half, 7, 5),
            (turn(o, 6), 0, half, 2, 4),
            (turn(o, 2), half, half, 6, 0),
        )
        return [
            (
                sem,
                pltpu.make_async_remote_copy(
                    src_ref=proj[chunk].at[source, pl.ds(low, size)],
                    dst_ref=proj[chunk].at[source, pl.ds(low, size)],
                    send_sem=ps.at[chunk, sem],
                    recv_sem=pr.at[chunk, sem],
                    device_id={"opt": turn(o, k)},
                    device_id_type=MESH,
                ),
            )
            for source, low, size, k, sem in moves
        ]

    waiting = loads[2:5]

    def weights():
        while waiting:
            waiting.pop(0).wait()

    def project(chunk):
        weights()
        for q in range(*CHUNKS[chunk]):
            moving.arrived(("token", q))
        rows = trecv[chunk][...].reshape(rows_of(chunk), MODEL)
        local = pl.ds(0, rows_of(chunk))
        for part in range(3):
            columns = pl.ds(part * 256, 256)
            gate = jnp.dot(rows, gate_v[:, columns], preferred_element_type=F32)
            up = jnp.dot(rows, up_v[:, columns], preferred_element_type=F32)
            hidden[local, columns] = (gate / (1.0 + jnp.exp(-gate)) * up).astype(BF16)
        projected = jnp.dot(hidden[local, :], basis_v[...], preferred_element_type=F32)
        proj[chunk][o] = projected.astype(BF16)

    def send_direct(chunk):
        for k in DIRECT:
            moving.start(("proj", chunk, k), direct(chunk, k))

    def hop(chunk, stage):
        size = rows_of(chunk)
        half = size // 2 if stage == 3 else size
        moving.arrived(("proj", chunk, stage))
        moving.arrived(("proj", chunk, 8 - stage))
        for source, low, k, sem in (
            (turn(o, 8 - stage), 0, 1, stage + 1),
            (turn(o, stage), size - half, 7, 0 if stage == 3 else 7 - stage),
        ):
            piece = proj[chunk].at[source, pl.ds(low, half)]
            copy = pltpu.make_async_remote_copy(
                src_ref=piece,
                dst_ref=piece,
                send_sem=ps.at[chunk, sem],
                recv_sem=pr.at[chunk, sem],
                device_id={"opt": turn(o, k)},
                device_id_type=MESH,
            )
            moving.start(("proj", chunk, sem), copy)

    def pass_on(chunk):
        moving.arrived(("proj", chunk, 2))
        moving.arrived(("proj", chunk, 6))
        for sem, copy in forwards(chunk):
            moving.start(("proj", chunk, sem), copy)

    def contract(chunk):
        for q in range(*CHUNKS[chunk]):
            moving.arrived(("cot", q))
        for k in range(8):
            moving.arrived(("proj", chunk, k))
        term = lax.dot_general(
            proj[chunk][...].reshape(8 * rows_of(chunk), RANK),
            crecv[chunk][...].reshape(8 * rows_of(chunk), FEAT),
            (((0,), (0,)), ((), ())),
            preferred_element_type=F32,
        )
        grad[...] = term if chunk == 0 else grad[...] + term

    def send_cots():
        for q in COT_LATER:
            send_cot(q)

    run = {
        "tokens": send_tokens,
        "project": project,
        "hop": hop,
        "direct": send_direct,
        "pass": pass_on,
        "cot": send_cots,
        "grad": contract,
    }
    for step, *where in SCHEDULE:
        run[step](*where)
    weights()
    gsend[...] = grad[...].astype(BF16)

    def part_rows(owner, part):
        return pl.ds(pl.multiple_of(owner * OWN + part * PART, PART), PART)

    def grad_copy(k, part):
        return pltpu.make_async_remote_copy(
            src_ref=gsend.at[part_rows(turn(r, k), part)],
            dst_ref=grecv.at[k, pl.ds(part * PART, PART)],
            send_sem=gs.at[part, k],
            recv_sem=gr.at[part, k],
            device_id={"rep": turn(r, k)},
            device_id_type=MESH,
        )

    def update_copy(k, part):
        rows = part_rows(r, part)
        return pltpu.make_async_remote_copy(
            src_ref=upd.at[rows],
            dst_ref=upd.at[rows],
            send_sem=us.at[part, k],
            recv_sem=ur.at[part, k],
            device_id={"rep": turn(r, k)},
            device_id_type=MESH,
        )

    for part in range(PARTS):
        for k in REP_HOPS:
            moving.start(("grad", k, part), grad_copy(k, part))
    loads[5].wait()
    loads[6].wait()
    for part in range(PARTS):
        local = pl.ds(part * PART, PART)
        rows = part_rows(r, part)
        gradient = grad[rows, :]
        for k in REP_HOPS:
            moving.arrived(("grad", k, part))
        for k in REP_HOPS:
            gradient += grecv[k, local].astype(F32)
        gradient_out[local, :] = gradient
        upd[rows, :] = adam(m1_v[local, :], m2_v[local, :], gradient)[2]
        for k in REP_HOPS:
            moving.start(("update", k, part), update_copy(k, part))
    moving.finish()
    update_out[...] = upd[...]


def finish(gradient_ref, update_ref, basis_ref, m1_ref, m2_ref, m1_out, m2_out, delta_out):
    first_moment, second_moment, _ = adam(m1_ref[0], m2_ref[0], gradient_ref[...])
    m1_out[0] = first_moment
    m2_out[0] = second_moment
    delta_out[0] = jnp.dot(basis_ref[0], update_ref[...], preferred_element_type=F32).astype(BF16)


def shards(
    incoming_tokens,
    cotangent,
    block_dest,
    gate_weight,
    up_weight,
    basis,
    moment_first,
    moment_second,
):
    tokens = incoming_tokens.reshape(BLOCKS, 8, SUB, FEAT)
    cot = cotangent.reshape(BLOCKS, 8, SUB, FEAT)
    hbm = pl.BlockSpec(memory_space=pl.ANY)
    vmem = pl.BlockSpec(memory_space=pltpu.VMEM)
    dma = pltpu.SemaphoreType.DMA
    gradient, update = pl.pallas_call(
        kernel,
        out_shape=(
            jax.ShapeDtypeStruct((OWN, FEAT), F32),
            jax.ShapeDtypeStruct((RANK, FEAT), BF16),
        ),
        in_specs=[pl.BlockSpec(memory_space=pltpu.SMEM)] + [hbm] * 7,
        out_specs=(vmem, vmem),
        scratch_shapes=[
            pltpu.VMEM((MODEL, FF), BF16),
            pltpu.VMEM((MODEL, FF), BF16),
            pltpu.VMEM((FF, RANK), BF16),
            pltpu.VMEM((BLOCKS, 8, SUB, FEAT), BF16),
            pltpu.VMEM((OWN, FEAT), F32),
            pltpu.VMEM((OWN, FEAT), F32),
            pltpu.VMEM((BLOCKS, SUB, MODEL), BF16),
            pltpu.VMEM((16, 8, SUB, FEAT), BF16),
            pltpu.VMEM((16, SUB, MODEL), BF16),
            pltpu.VMEM((rows_of(0), FF), BF16),
            pltpu.VMEM((RANK, FEAT), F32),
            pltpu.VMEM((RANK, FEAT), BF16),
            pltpu.VMEM((8, OWN, FEAT), BF16),
            pltpu.VMEM((RANK, FEAT), BF16),
            [pltpu.VMEM((8, high - low, SUB, FEAT), BF16) for low, high in CHUNKS],
            [pltpu.VMEM((high - low, SUB, MODEL), BF16) for low, high in CHUNKS],
            [pltpu.VMEM((8, (high - low) * SUB, RANK), BF16) for low, high in CHUNKS],
            dma((7,)),
            dma((8,)), dma((8,)),
            dma((16,)), dma((16,)),
            dma((16,)), dma((16,)),
            dma((len(CHUNKS), 8)), dma((len(CHUNKS), 8)),
            dma((PARTS, 8)), dma((PARTS, 8)),
            dma((PARTS, 8)), dma((PARTS, 8)),
        ],
        compiler_params=pltpu.CompilerParams(
            collective_id=0, has_side_effects=True, vmem_limit_bytes=63 * 1024 * 1024
        ),
    )(
        jnp.transpose(block_dest, (1, 2, 0)),
        tokens,
        cot,
        gate_weight,
        up_weight,
        basis,
        moment_first,
        moment_second,
    )
    return pl.pallas_call(
        finish,
        out_shape=(
            jax.ShapeDtypeStruct((1, OWN, FEAT), F32),
            jax.ShapeDtypeStruct((1, OWN, FEAT), F32),
            jax.ShapeDtypeStruct((1, FF, FEAT), BF16),
        ),
        in_specs=[vmem] * 5,
        out_specs=(vmem, vmem, vmem),
        cost_estimate=pl.CostEstimate(flops=2 * FF * RANK * FEAT, bytes_accessed=2**21, transcendentals=0),
    )(gradient, update, basis, moment_first, moment_second)


def solution(mesh):
    in_specs = (
        P("ep", "rep", None, None, "opt"),
        P("ep", "rep", None, None, "opt"),
        P(),
        P("ep", None, None),
        P("ep", None, None),
        P("ep", None, None),
        P("ep", "rep", "opt"),
        P("ep", "rep", "opt"),
    )
    out_specs = (P("ep", "rep", "opt"), P("ep", "rep", "opt"), P("ep", None, "opt"))
    return jax.shard_map(shards, mesh=mesh, in_specs=in_specs, out_specs=out_specs, check_vma=False)
```
